512 devices in a mesh: dp: 128 (over z, y_lo, x), cls: 4 (over y_hi, core).
Axes of the slice: x: 4, y: 8 (y_hi: 2, y_lo: 4; y = y_hi * 4 + y_lo), z: 8, core: 2. Of those that a mesh axis runs over, the one named last changes fastest.
Arguments:
- particles: bfloat16 [16384, 64, 2, 128], P('dp', 'cls'), may hold values from -20 to 20
- transfer_group: int32 [16384], P('dp'), may hold values from 0 to 63
- counts: int32 [128], P('dp'), may hold values from 0 to 128, as said below
- routing: int32 [16384, 2], P('dp'), may hold values from 0 to 127, as said below
- references: bfloat16 [256, 16384], P('cls', 'dp'), may hold values from -2 to 2
- ctf_table: float32 [64, 64], replicated, may hold values from 0.2 to 1
- noise_weight: float32 [64], replicated, may hold values from 0.05 to 0.5
- rotation_index: int32 [64], replicated, may hold values from 0 to 127, as said below
Outputs:
- log_normalizer: float32 [8192], P('dp')
- class_sums: float32 [256, 16384], P('cls', 'dp')
The draws below stay inside these ranges and needn't reach their ends.
Inputs may be any that keep to these rules, and one draw needn't show every extreme that they name: The live slots of an index of dp are its first counts slots; counts sum to 8192. `routing`: for a live slot, the index of dp and the slot of its particle in the rebalanced order; the live slots fill every index's 64 slots exactly once; one index of dp sends at most 1 particles to any one index, and some index sends exactly 1 to some index; entries of slots that are not live are 0. `rotation_index`: 64 distinct angular shifts, in units of one of the 128 angles.
All inputs are finite; a program needn't handle non-finite values.
Results may differ from the reference program's by a relative error of at most 0.0087.
Values may be sent and summed in bfloat16 or wider, within the bound.
No kernel may reach another device: no remote copies, remote signals or barrier semaphores. Data moves between devices by JAX's collectives and lax.ppermute only.
A program may use at most 128 MiB of HBM per device.

```python
import math
import jax
import jax.numpy as jnp
from jax import lax

R = 64
A = 128
CLASSES = 256
NROT = 64
TRANSFER_GROUPS = 64
PART_DEV = 64
SLOTS = 128
NPART = 8192
TOTAL_SLOTS = 16384
N_DP = 128


def template_images(key):
    samples = jax.random.normal(jax.random.fold_in(key, 3), (CLASSES, R, 2, A), jnp.float32)
    return jnp.clip(samples, -3.0, 3.0) * (12.8 / (2.0 * R * A) ** 0.5)


def chosen_angles(key):
    random_ints = jax.random.randint(jax.random.fold_in(key, 5), (A,), 0, 1 << 20)
    scores = random_ints * A + lax.iota(jnp.int32, A)
    return jnp.argsort(scores)[:NROT].astype(jnp.int32)


def plan_routes(key):
    pair_count = N_DP // 2
    imbalance = jax.random.randint(jax.random.fold_in(key, 7), (pair_count,), -(PART_DEV // 2), PART_DEV // 2 + 1)
    imbalance = imbalance.at[0].set(PART_DEV)
    counts = jnp.stack([PART_DEV + imbalance, PART_DEV - imbalance], axis=1).reshape(N_DP).astype(jnp.int32)
    slot_ids = lax.iota(jnp.int32, SLOTS)
    empty_slots = slot_ids[None, :] >= counts[:, None]
    random_ints = jax.random.randint(jax.random.fold_in(key, 9), (N_DP, SLOTS), 0, 1 << 20)
    scores = random_ints * SLOTS + slot_ids[None, :] + empty_slots.astype(jnp.int32) * (1 << 30)
    ranking = jnp.argsort(jnp.argsort(scores, axis=1), axis=1).astype(jnp.int32)
    offsets = jnp.cumsum(counts) - counts
    global_rank = offsets[:, None] + ranking
    target_device = jnp.where(empty_slots, 0, global_rank % N_DP)
    target_slot = jnp.where(empty_slots, 0, global_rank // N_DP)
    routing = jnp.stack([target_device, target_slot], axis=-1).reshape(N_DP * SLOTS, 2).astype(jnp.int32)
    return (counts, routing)


def draw_counts(key, part):
    return plan_routes(key)[0]


def draw_routing(key, part):
    return plan_routes(key)[1]


def draw_references(key, part):
    return template_images(key).reshape(CLASSES, R * 2 * A).astype(jnp.bfloat16)


def draw_rotation_index(key, part):
    return chosen_angles(key)


def draw_particles(key, part):
    row_total = N_DP * SLOTS
    samples = jnp.clip(jax.random.normal(jax.random.fold_in(key, 11), (row_total, R, 2, A), jnp.float32), -6.0, 6.0)
    return jnp.clip(samples, -20.0, 20.0).astype(jnp.bfloat16)


def with_ends(entries, key, smallest, high):
    index_at = [jax.random.randint(jax.random.fold_in(key, axis), (), 0, length) for axis, length in enumerate(entries.shape)]
    widest = entries.shape.index(max(entries.shape))
    neighbour = index_at[:widest] + [(index_at[widest] + 1) % entries.shape[widest]] + index_at[widest + 1:]
    return entries.at[tuple(index_at)].set(smallest).at[tuple(neighbour)].set(high)


def setup_inputs(seed: int = 0) -> dict:
    arg_keys = jax.random.split(jax.random.key(seed), 9)
    return {
        "particles": draw_particles(jax.random.fold_in(arg_keys[8], 71), 0),
        "transfer_group": with_ends(jax.random.randint(arg_keys[1], (TOTAL_SLOTS,), 0, TRANSFER_GROUPS), jax.random.fold_in(arg_keys[1], 1), 0, TRANSFER_GROUPS - 1).astype(jnp.int32),
        "counts": draw_counts(jax.random.fold_in(arg_keys[8], 71), 0),
        "routing": draw_routing(jax.random.fold_in(arg_keys[8], 71), 0),
        "references": draw_references(jax.random.fold_in(arg_keys[8], 71), 0),
        "ctf_table": jnp.clip(jax.random.uniform(arg_keys[5], (TRANSFER_GROUPS, R), jnp.float32, 0.2, 1.0), 0.2, 1.0),
        "noise_weight": jnp.clip(jnp.exp(jax.random.uniform(arg_keys[6], (R,), jnp.float32, math.log(0.05), math.log(0.5))), 0.05, 0.5),
        "rotation_index": draw_rotation_index(jax.random.fold_in(arg_keys[8], 71), 0),
    }


def angle_tables(length, shifts):
    phases = (lax.iota(jnp.int32, length)[:, None] * shifts[None, :]) % length
    angles = phases.astype(jnp.float32) * (2.0 * math.pi / length)
    return jnp.cos(angles), jnp.sin(angles)


def forward_table(length):
    cosine_terms, sine_part = angle_tables(length, lax.iota(jnp.int32, length))
    upper_half = jnp.concatenate([cosine_terms, -sine_part], axis=1)
    lower_half = jnp.concatenate([sine_part, cosine_terms], axis=1)
    return jnp.concatenate([upper_half, lower_half], axis=0)


def inverse_table(length):
    cosine_terms, sine_part = angle_tables(length, lax.iota(jnp.int32, length))
    upper_half = jnp.concatenate([cosine_terms, sine_part], axis=1)
    lower_half = jnp.concatenate([-sine_part, cosine_terms], axis=1)
    return jnp.concatenate([upper_half, lower_half], axis=0) / length


def shift_tables(rotation_index):
    cosine_terms, sine_part = angle_tables(A, rotation_index)
    stacked = jnp.concatenate([cosine_terms, sine_part], axis=0)
    return stacked / A, stacked.T


def cycle_spectra(images, cycle_scale, forward):
    batch_rows, cycle_count = images.shape[0], images.shape[1]
    flattened = images.reshape(batch_rows * cycle_count, -1).astype(jnp.float32)
    spectrum = jnp.dot(flattened, forward, precision=lax.Precision.HIGHEST)
    spectrum = spectrum.reshape(batch_rows, cycle_count, -1) * cycle_scale[:, :, None]
    return spectrum.astype(jnp.bfloat16)


def class_spectra(gathered, forward):
    class_count = gathered.shape[0]
    flattened = gathered.reshape(class_count * R, 2 * A).astype(jnp.float32)
    cycle_power = jnp.sum(flattened * flattened, axis=1).reshape(class_count, R)
    transform = jnp.dot(flattened, forward, precision=lax.Precision.HIGHEST)
    transform = transform.astype(jnp.bfloat16).reshape(class_count, R, 2 * A)
    real_part = transform[:, :, :A]
    imag_part = transform[:, :, A:]
    first_block = jnp.concatenate([real_part, imag_part], axis=1)
    second_block = jnp.concatenate([imag_part, -real_part], axis=1)
    class_matrix = jnp.transpose(jnp.concatenate([first_block, second_block], axis=0), (2, 1, 0))
    return class_matrix, cycle_power


def correlate(spectrum, penalty_weight, class_matrix, cycle_power, forward_shifted):
    batch_rows = spectrum.shape[0]
    class_count = cycle_power.shape[0]
    stacked = jnp.transpose(spectrum.reshape(batch_rows, R, 2, A), (3, 0, 2, 1)).reshape(A, batch_rows, 2 * R)
    cross_terms = jnp.einsum("mbr,mrc->mbc", stacked.astype(jnp.float32), class_matrix.astype(jnp.float32), precision=lax.Precision.HIGHEST)
    flattened = jnp.transpose(cross_terms.reshape(A, batch_rows, 2, class_count), (1, 3, 2, 0)).reshape(batch_rows * class_count, 2 * A)
    penalty = 0.5 * jnp.dot(penalty_weight, cycle_power.T, precision=lax.Precision.HIGHEST)
    scores = jnp.dot(flattened, forward_shifted, precision=lax.Precision.HIGHEST).reshape(batch_rows, class_count, -1)
    return scores - penalty[:, :, None]


def backproject(responsibility, spectrum, shift_back):
    batch_rows, class_count = responsibility.shape[0], responsibility.shape[1]
    angular = jnp.dot(responsibility.reshape(batch_rows * class_count, -1).astype(jnp.float32), shift_back, precision=lax.Precision.HIGHEST)
    angular = angular.astype(jnp.bfloat16).reshape(batch_rows, class_count, 2, A)
    real_part = angular[:, :, 0, :]
    imag_part = angular[:, :, 1, :]
    left_side = jnp.concatenate([jnp.concatenate([real_part, -imag_part], axis=0), jnp.concatenate([imag_part, real_part], axis=0)], axis=1)
    left_side = jnp.transpose(left_side, (2, 1, 0))
    right_factor = jnp.transpose(spectrum.reshape(batch_rows, R, 2, A), (3, 2, 0, 1)).reshape(A, 2 * batch_rows, R)
    return jnp.einsum("mkb,mbr->mkr", left_side.astype(jnp.float32), right_factor.astype(jnp.float32), precision=lax.Precision.HIGHEST)


def class_images(partial_value, inverse):
    class_count = partial_value.shape[1] // 2
    ordered = jnp.transpose(partial_value.reshape(A, 2, class_count, R), (2, 3, 1, 0)).reshape(class_count * R, 2 * A)
    result = jnp.dot(ordered, inverse, precision=lax.Precision.HIGHEST)
    return result.reshape(class_count, R * 2 * A)


def reference(particles, transfer_group, counts, routing, references, ctf_table, noise_weight, rotation_index):
    slot_total = particles.shape[0]
    slot_count = slot_total // N_DP
    slot_ids = lax.iota(jnp.int32, slot_total)
    live_slots = (slot_ids % slot_count) < counts[slot_ids // slot_count]
    destination = jnp.where(live_slots, routing[:, 0] * PART_DEV + routing[:, 1], NPART).astype(jnp.int32)
    images = jnp.zeros((NPART, R, 2, A), jnp.bfloat16).at[destination].set(particles, mode="drop")
    group_ids = jnp.zeros((NPART,), jnp.int32).at[destination].set(transfer_group, mode="drop")
    ctf_values = ctf_table[group_ids]
    cycle_scale = ctf_values * noise_weight[None, :]
    penalty_weight = cycle_scale * ctf_values
    forward = forward_table(A)
    class_matrix, cycle_power = class_spectra(references, forward)
    forward_shifted, shift_back = shift_tables(rotation_index)
    block_rows = math.gcd(NPART, 256)
    block_total = NPART // block_rows
    image_blocks = images.reshape(block_total, block_rows, R, 2, A)
    scale_blocks = cycle_scale.reshape(block_total, block_rows, R)
    weight_blocks = penalty_weight.reshape(block_total, block_rows, R)

    def one_block(running, inputs):
        block_images, scale_per_block, block_weight = inputs
        spectrum = cycle_spectra(block_images, scale_per_block, forward)
        scores = correlate(spectrum, block_weight, class_matrix, cycle_power, forward_shifted)
        peak_score = jnp.max(scores, axis=(1, 2))
        sum_exp = jnp.sum(jnp.exp(scores - peak_score[:, None, None]), axis=(1, 2))
        log_norm = peak_score + jnp.log(sum_exp)
        responsibility = jnp.exp(scores - log_norm[:, None, None]).astype(jnp.bfloat16)
        return running + backproject(responsibility, spectrum, shift_back), log_norm

    initial = jnp.zeros((A, 2 * CLASSES, R), jnp.float32)
    totals, norms = lax.scan(one_block, initial, (image_blocks, scale_blocks, weight_blocks))
    return norms.reshape(NPART), class_images(totals, inverse_table(A))
```

```python
import functools
import math

import jax
import jax.numpy as jnp
from jax import lax
from jax.sharding import PartitionSpec as P

R = 64
A = 128
PART_DEV = 64
N_DP = 128
X_SIZE = 4


def angle_tables(length, shifts):
    phases = lax.iota(jnp.int32, length)[:, None] * shifts[None, :] % length
    angles = phases.astype(jnp.float32) * (2.0 * math.pi / length)
    return (jnp.cos(angles), jnp.sin(angles))


def forward_table(length):
    cosine_terms, sine_part = angle_tables(length, lax.iota(jnp.int32, length))
    upper_half = jnp.concatenate([cosine_terms, -sine_part], axis=1)
    lower_half = jnp.concatenate([sine_part, cosine_terms], axis=1)
    return jnp.concatenate([upper_half, lower_half], axis=0)


def inverse_table(length):
    cosine_terms, sine_part = angle_tables(length, lax.iota(jnp.int32, length))
    upper_half = jnp.concatenate([cosine_terms, sine_part], axis=1)
    lower_half = jnp.concatenate([-sine_part, cosine_terms], axis=1)
    return jnp.concatenate([upper_half, lower_half], axis=0) / length


def shift_tables(rotation_index):
    cosine_terms, sine_part = angle_tables(A, rotation_index)
    stacked = jnp.concatenate([cosine_terms, sine_part], axis=0)
    return (stacked / A, stacked.T)


def cycle_spectra(images, cycle_scale, forward):
    batch_rows, cycle_count = (images.shape[0], images.shape[1])
    flattened = images.reshape(batch_rows * cycle_count, -1).astype(jnp.float32)
    spectrum = jnp.dot(flattened, forward, precision=lax.Precision.HIGHEST)
    spectrum = spectrum.reshape(batch_rows, cycle_count, -1) * cycle_scale[:, :, None]
    return spectrum.astype(jnp.bfloat16)


def class_spectra(gathered, forward):
    class_count = gathered.shape[0]
    flattened = gathered.reshape(class_count * R, 2 * A).astype(jnp.float32)
    cycle_power = jnp.sum(flattened * flattened, axis=1).reshape(class_count, R)
    transform = jnp.dot(flattened, forward, precision=lax.Precision.HIGHEST)
    transform = transform.astype(jnp.bfloat16).reshape(class_count, R, 2 * A)
    real_part = transform[:, :, :A]
    imag_part = transform[:, :, A:]
    first_block = jnp.concatenate([real_part, imag_part], axis=1)
    second_block = jnp.concatenate([imag_part, -real_part], axis=1)
    class_matrix = jnp.transpose(jnp.concatenate([first_block, second_block], axis=0), (2, 1, 0))
    return (class_matrix, cycle_power)


def correlate(spectrum, penalty_weight, class_matrix, cycle_power, forward_shifted):
    batch_rows = spectrum.shape[0]
    class_count = cycle_power.shape[0]
    stacked = jnp.transpose(spectrum.reshape(batch_rows, R, 2, A), (3, 0, 2, 1)).reshape(
        A, batch_rows, 2 * R
    )
    cross_terms = jnp.einsum(
        "mbr,mrc->mbc", stacked, class_matrix, preferred_element_type=jnp.float32
    )
    flattened = jnp.transpose(
        cross_terms.reshape(A, batch_rows, 2, class_count), (1, 3, 2, 0)
    ).reshape(batch_rows * class_count, 2 * A)
    penalty = 0.5 * jnp.dot(penalty_weight, cycle_power.T, precision=lax.Precision.HIGHEST)
    scores = jnp.dot(flattened, forward_shifted, precision=lax.Precision.HIGHEST).reshape(
        batch_rows, class_count, -1
    )
    return scores - penalty[:, :, None]


def backproject(responsibility, spectrum, shift_back):
    batch_rows, class_count = (responsibility.shape[0], responsibility.shape[1])
    angular = jnp.dot(
        responsibility.reshape(batch_rows * class_count, -1).astype(jnp.float32),
        shift_back,
        precision=lax.Precision.HIGHEST,
    )
    angular = angular.astype(jnp.bfloat16).reshape(batch_rows, class_count, 2, A)
    real_part = angular[:, :, 0, :]
    imag_part = angular[:, :, 1, :]
    left_side = jnp.concatenate(
        [
            jnp.concatenate([real_part, -imag_part], axis=0),
            jnp.concatenate([imag_part, real_part], axis=0),
        ],
        axis=1,
    )
    left_side = jnp.transpose(left_side, (2, 1, 0))
    right_factor = jnp.transpose(spectrum.reshape(batch_rows, R, 2, A), (3, 2, 0, 1)).reshape(
        A, 2 * batch_rows, R
    )
    return jnp.einsum("mkb,mbr->mkr", left_side, right_factor, preferred_element_type=jnp.float32)


def class_images(partial_value, inverse):
    class_count = partial_value.shape[1] // 2
    ordered = jnp.transpose(partial_value.reshape(A, 2, class_count, R), (2, 3, 1, 0)).reshape(
        class_count * R, 2 * A
    )
    result = jnp.dot(ordered, inverse, precision=lax.Precision.HIGHEST)
    return result.reshape(class_count, R * 2 * A)


def axis_groups():
    rows = N_DP // X_SIZE
    along_x = [[row * X_SIZE + x for x in range(X_SIZE)] for row in range(rows)]
    across_x = [[row * X_SIZE + x for row in range(rows)] for x in range(X_SIZE)]
    return along_x, across_x


def route_particles(particles, transfer_group, counts, routing):
    slot_count = particles.shape[0]
    image_shape = particles.shape[1:]
    slot_ids = lax.iota(jnp.int32, slot_count)
    live_slots = slot_ids < counts[0]
    matches = (
        lax.iota(jnp.int32, N_DP)[:, None] == routing[:, 0][None, :]
    ) & live_slots[None, :]
    chosen = matches.astype(jnp.bfloat16)
    rows = jnp.dot(
        chosen, particles.reshape(slot_count, -1), preferred_element_type=jnp.float32
    ).astype(jnp.bfloat16)
    sent_slot = jnp.sum(jnp.where(matches, routing[:, 1][None, :] + 1, 0), axis=1)
    sent_group = jnp.sum(jnp.where(matches, transfer_group[None, :], 0), axis=1)
    lanes = lax.iota(jnp.int32, A)[None, :]
    tags = jnp.where(lanes == 0, sent_slot[:, None], jnp.where(lanes == 1, sent_group[:, None], 0))
    outgoing = jnp.concatenate(
        [rows.reshape(N_DP, -1, A), tags.astype(jnp.bfloat16)[:, None, :]], axis=1
    )
    arrived = lax.all_to_all(outgoing, "dp", split_axis=0, concat_axis=0, tiled=True)
    row_count = outgoing.shape[1] - 1
    arrived_slot = arrived[:, row_count, 0].astype(jnp.int32) - 1
    arrived_group = arrived[:, row_count, 1].astype(jnp.int32)
    placed = lax.iota(jnp.int32, PART_DEV)[:, None] == arrived_slot[None, :]
    images = jnp.dot(
        placed.astype(jnp.bfloat16),
        arrived[:, :row_count].reshape(N_DP, -1),
        preferred_element_type=jnp.float32,
    ).astype(jnp.bfloat16)
    group_ids = jnp.sum(jnp.where(placed, arrived_group[None, :], 0), axis=1)
    return images.reshape((PART_DEV,) + image_shape), group_ids


def gather_cycles(images):
    far = lax.ppermute(images, "cls", [(i, i ^ 2) for i in range(4)])
    mine_high = lax.axis_index("cls") // 2 == 1
    mine_odd = lax.axis_index("cls") % 2 == 1
    column = jnp.stack([jnp.where(mine_high, far, images), jnp.where(mine_high, images, far)])
    near = lax.ppermute(column, "cls", [(i, i ^ 1) for i in range(4)])
    both = jnp.stack(
        [jnp.where(mine_odd, near, column), jnp.where(mine_odd, column, near)], axis=1
    )
    return jnp.transpose(both, (2, 0, 1, 3, 4, 5)).reshape(PART_DEV, R, 2, A)


def gather_references(references):
    along_x, across_x = axis_groups()
    rows = N_DP // X_SIZE
    block = jnp.broadcast_to(references[None], (rows,) + references.shape)
    block = lax.all_to_all(block, "dp", 0, 0, axis_index_groups=across_x, tiled=True)
    block = jnp.broadcast_to(block[None], (X_SIZE,) + block.shape)
    return lax.all_to_all(block, "dp", 0, 0, axis_index_groups=along_x, tiled=True)


def scatter_sums(blocks):
    along_x, across_x = axis_groups()
    arrived = lax.all_to_all(blocks, "dp", 0, 0, axis_index_groups=along_x, tiled=True)
    partial_sum = jnp.sum(arrived.astype(jnp.float32), axis=0).astype(jnp.bfloat16)
    arrived = lax.all_to_all(partial_sum, "dp", 0, 0, axis_index_groups=across_x, tiled=True)
    return jnp.sum(arrived.astype(jnp.float32), axis=0)


def join_normalizer(local_peak, local_sum):
    mine = jnp.stack([local_peak, local_sum])
    all_parts = [mine] + [
        lax.ppermute(mine, "cls", [(i, i ^ k) for i in range(4)]) for k in (1, 2, 3)
    ]
    peak = functools.reduce(jnp.maximum, [part[0] for part in all_parts])
    order = lax.axis_index("cls")
    by_offset = jnp.stack([part[1] * jnp.exp(part[0] - peak) for part in all_parts])
    by_owner = [lax.dynamic_index_in_dim(by_offset, order ^ i, 0, keepdims=False) for i in range(4)]
    return peak + jnp.log(by_owner[0] + by_owner[1] + by_owner[2] + by_owner[3])


def local(
    particles, transfer_group, counts, routing, references, ctf_table, noise_weight, rotation_index
):
    gathered = gather_references(references)
    images, group_ids = route_particles(particles, transfer_group, counts, routing)
    whole_images = gather_cycles(images)
    group_hits = (group_ids[:, None] == lax.iota(jnp.int32, ctf_table.shape[0])[None, :]).astype(
        jnp.float32
    )
    ctf_values = jnp.dot(group_hits, ctf_table, precision=lax.Precision.HIGHEST)
    cycle_scale = ctf_values * noise_weight[None, :]
    penalty_weight = cycle_scale * ctf_values
    forward = forward_table(A)
    rows = N_DP // X_SIZE
    flat_references = jnp.transpose(gathered, (2, 1, 0, 3)).reshape(-1, R * 2 * A)
    class_matrix, cycle_power = class_spectra(flat_references, forward)
    forward_shifted, shift_back = shift_tables(rotation_index)
    spectrum = cycle_spectra(whole_images, cycle_scale, forward)
    scores = correlate(spectrum, penalty_weight, class_matrix, cycle_power, forward_shifted)
    local_peak = jnp.max(scores, axis=(1, 2))
    local_sum = jnp.sum(jnp.exp(scores - local_peak[:, None, None]), axis=(1, 2))
    log_norm = join_normalizer(local_peak, local_sum)
    responsibility = jnp.exp(scores - log_norm[:, None, None]).astype(jnp.bfloat16)
    partial_value = backproject(responsibility, spectrum, shift_back)
    local_sums = class_images(partial_value, inverse_table(A)).astype(jnp.bfloat16)
    class_count = local_sums.shape[0]
    blocks = jnp.transpose(local_sums.reshape(class_count, rows, X_SIZE, A), (2, 1, 0, 3))
    return (log_norm, scatter_sums(blocks))


def solution(mesh):
    return jax.shard_map(
        local,
        mesh=mesh,
        in_specs=(
            P("dp", "cls", None, None),
            P("dp"),
            P("dp"),
            P("dp", None),
            P("cls", "dp"),
            P(),
            P(),
            P(),
        ),
        out_specs=(P("dp"), P("cls", "dp")),
        check_vma=False,
    )
```
